32 devices in a mesh: group: 2 (over y), dp: 8 (over z, x), tensor: 2 (over core).
Axes of the slice: x: 2, y: 2, z: 4, core: 2. Of those that a mesh axis runs over, the one named last changes fastest.
Arguments:
- queries: bfloat16 [2048, 8, 4096], P(('group', 'dp'), None, 'tensor'), parts along dimension 0, may hold values from -6 to 6
- key_value_pairs: bfloat16 [2048, 8, 1024], P(('group', 'dp'), None, 'tensor'), parts along dimension 0, may hold values from -6 to 6
- prompt_cache: bfloat16 [2048, 1024], P('group', 'tensor'), parts along dimension 0, may hold values from -6 to 6
- score_weight: bfloat16 [4096], P('tensor'), may hold values from -4 to 4
- old_values: float32 [2048, 8], P(('group', 'dp')), parts along dimension 0, may hold values from -6 to 6
- lengths: int32 [2048], P('group'), parts along dimension 0, may hold values from 1 to 8, as said below
- target_rank: int32 [2048], P('group'), parts along dimension 0, may hold values from 0 to 7, as said below
Outputs:
- attention: bfloat16 [2048, 8, 4096], P(('group', 'dp'), None, 'tensor'), parts along dimension 0
- score_delta: float32 [2048, 8], P(('group', 'dp')), parts along dimension 0
The draws below stay inside these ranges and needn't reach their ends.
There are 2 independent parts, one for each index of `group`. The reference program is written for one: setup_inputs(seed, part) draws one part's arguments, and reference() takes and returns one part's arrays. A program takes and returns all parts, laid end to end along the dimension named above; an argument that names none is the same for every part. Nothing has to cross between parts.
Inputs may be any that keep to these rules, and one draw needn't show every extreme that they name: `lengths`: some response has exactly 8 tokens in every draw. `target_rank`: for every slot index t, the t-th responses of the 8 indices of dp go to 8 different indices, so every index receives one response for each slot index. Two indices of dp that send one another any responses send exactly 16.
All inputs are finite; a program needn't handle non-finite values.
Results may differ from the reference program's by a relative error of at most 0.0047.
Values may be sent and summed in bfloat16 or wider, within the bound.
A program may use at most 128 MiB of HBM per device.

```python
import jax
import jax.numpy as jnp
from jax import lax

HQ = 32
KEY_VALUE_HEADS = 4
HEAD_SIZE = 128
SEQ_DEV = 128
SLOT_TOKENS = 8
PROMPT_TOKENS = 1024
RESPONSE_SLOTS = 1024


def draw_queries(key, part):
    key = jax.random.fold_in(key, 11)
    complete_shape = (RESPONSE_SLOTS, SLOT_TOKENS, HQ * HEAD_SIZE)
    base_sample = jnp.clip(jax.random.normal(key, complete_shape, jnp.float32), -6.0, 6.0)
    return base_sample.astype(jnp.bfloat16)


def draw_prompt_cache(key, part):
    key = jax.random.fold_in(key, 13)
    complete_shape = (PROMPT_TOKENS, KEY_VALUE_HEADS, 2, HEAD_SIZE)
    base_sample = jnp.clip(jax.random.normal(key, complete_shape, jnp.float32), -6.0, 6.0)
    return base_sample.reshape(PROMPT_TOKENS, KEY_VALUE_HEADS * 2 * HEAD_SIZE).astype(jnp.bfloat16)


def draw_lengths(key, part):
    key = jax.random.fold_in(key, 21)
    first_key, second_key, third_key = jax.random.split(key, 3)
    rank_total = RESPONSE_SLOTS // SEQ_DEV
    longest = jax.random.randint(first_key, (rank_total,), max(1, SLOT_TOKENS // 4), SLOT_TOKENS + 1)
    bounds = jnp.repeat(longest, SEQ_DEV)
    drawn_lens = 1 + jax.random.randint(second_key, (RESPONSE_SLOTS,), 0, bounds)
    chosen = jax.random.randint(third_key, (), 0, RESPONSE_SLOTS)
    return jnp.where(jnp.arange(RESPONSE_SLOTS) == chosen, SLOT_TOKENS, drawn_lens).astype(jnp.int32)


def draw_target_rank(key, part):
    key = jax.random.fold_in(key, 31)
    first_key, second_key, third_key = jax.random.split(key, 3)
    rank_total = RESPONSE_SLOTS // SEQ_DEV
    capacity = max(2, SEQ_DEV // rank_total)
    distinct = SEQ_DEV // capacity
    mixing = jax.random.permutation(first_key, rank_total)
    inverse = jnp.argsort(mixing, stable=True)
    offsets = jax.random.permutation(second_key, rank_total)[:distinct]
    per_slot = offsets[jax.random.permutation(third_key, SEQ_DEV) // capacity]
    seq_index = jnp.arange(RESPONSE_SLOTS)
    source = seq_index // SEQ_DEV
    return mixing[(inverse[source] + per_slot[seq_index % SEQ_DEV]) % rank_total].astype(jnp.int32)


def level_of(stream_key, shape, cuts, smallest, high):
    def one(dim, shards_of):
        draws = jax.random.uniform(jax.random.fold_in(jax.random.fold_in(stream_key, 6), dim), (shards_of,), jnp.float32, smallest / len(cuts), high / len(cuts))
        return jnp.repeat(jnp.exp(draws), shape[dim] // shards_of).reshape((-1,) + (1,) * (len(shape) - dim - 1))

    loudness = one(*cuts[0])
    for cut in cuts[1:]:
        loudness = loudness * one(*cut)
    return loudness


def normal_values(key, extent, scale, bound, shards=(), kind=jnp.bfloat16):
    array = scale * jax.random.normal(key, extent, jnp.float32)
    if shards:
        array = array * level_of(key, extent, shards, -0.22, 0.18)
    return jnp.clip(array, -bound, bound).astype(kind)


def setup_inputs(seed: int = 0, part: int = 0) -> dict:
    seeds = jax.random.split(jax.random.key(seed), 8)
    own_keys = jax.random.split(jax.random.fold_in(seeds[7], part), 8)
    queries = draw_queries(jax.random.fold_in(jax.random.fold_in(seeds[7], part), 71), part)
    key_value_pairs = normal_values(own_keys[1], (RESPONSE_SLOTS, SLOT_TOKENS, KEY_VALUE_HEADS * 2 * HEAD_SIZE), 1.0, 6.0, ((0, 8), (2, 2)))
    prompt_cache = draw_prompt_cache(jax.random.fold_in(jax.random.fold_in(seeds[7], part), 71), part)
    score_weight = normal_values(seeds[3], (HQ * HEAD_SIZE,), 0.3, 4.0, ((0, 2),))
    old_values = normal_values(own_keys[4], (RESPONSE_SLOTS, SLOT_TOKENS), 1.0, 6.0, ((0, 8),), jnp.float32)
    lengths = draw_lengths(jax.random.fold_in(jax.random.fold_in(seeds[7], part), 71), part)
    target_rank = draw_target_rank(jax.random.fold_in(jax.random.fold_in(seeds[7], part), 71), part)
    return {"queries": queries, "key_value_pairs": key_value_pairs, "prompt_cache": prompt_cache, "score_weight": score_weight, "old_values": old_values, "lengths": lengths, "target_rank": target_rank}


def attend_block(queries, key_value_pairs, prompt_cache, seq_lens):
    blocks, slot_len, feature_width = queries.shape
    pair_heads = key_value_pairs.shape[2] // (2 * HEAD_SIZE)
    head_total = feature_width // HEAD_SIZE
    groups = head_total // pair_heads
    score_scale = HEAD_SIZE ** -0.5
    prompt_len = prompt_cache.shape[0]
    query_split = queries.astype(jnp.float32).reshape(blocks, slot_len, pair_heads, groups, HEAD_SIZE)
    own_pairs = key_value_pairs.astype(jnp.float32).reshape(blocks, slot_len, pair_heads, 2, HEAD_SIZE)
    cache_pairs = prompt_cache.astype(jnp.float32).reshape(prompt_len, pair_heads, 2, HEAD_SIZE)
    prompt_scores = jnp.einsum("bshgd,phd->bshgp", query_split, cache_pairs[:, :, 0]) * score_scale
    own_scores = jnp.einsum("bshgd,bthd->bshgt", query_split, own_pairs[:, :, :, 0]) * score_scale
    position = jnp.arange(slot_len)
    causal = position[None, :] <= position[:, None]
    own_scores = jnp.where(causal[None, :, None, None, :], own_scores, -1e30)
    row_top = jnp.maximum(jnp.max(prompt_scores, -1), jnp.max(own_scores, -1))
    prompt_exp = jnp.exp(prompt_scores - row_top[..., None])
    own_exp = jnp.exp(own_scores - row_top[..., None])
    denominator = jnp.sum(prompt_exp, -1) + jnp.sum(own_exp, -1)
    prompt_probs = lax.optimization_barrier(prompt_exp.astype(jnp.bfloat16)).astype(jnp.float32)
    own_probs = lax.optimization_barrier(own_exp.astype(jnp.bfloat16)).astype(jnp.float32)
    weighted = jnp.einsum("bshgp,phd->bshgd", prompt_probs, cache_pairs[:, :, 1])
    weighted = weighted + jnp.einsum("bshgt,bthd->bshgd", own_probs, own_pairs[:, :, :, 1])
    result = weighted / denominator[..., None]
    live_rows = position[None, :] < seq_lens[:, None]
    result = jnp.where(live_rows[:, :, None, None, None], result, 0.0)
    return result.reshape(blocks, slot_len, feature_width).astype(jnp.bfloat16)


def reference(queries, key_value_pairs, prompt_cache, score_weight, old_values, lengths, target_rank):
    block_sequences = min(RESPONSE_SLOTS, max(1, 512 // SLOT_TOKENS))
    step_count = RESPONSE_SLOTS // block_sequences

    def one_block(pieces):
        return attend_block(pieces[0], pieces[1], prompt_cache, pieces[2])

    attention_rows = lax.map(one_block, (
        queries.reshape(step_count, block_sequences, SLOT_TOKENS, HQ * HEAD_SIZE),
        key_value_pairs.reshape(step_count, block_sequences, SLOT_TOKENS, KEY_VALUE_HEADS * 2 * HEAD_SIZE),
        lengths.reshape(step_count, block_sequences)))
    attention_rows = attention_rows.reshape(RESPONSE_SLOTS, SLOT_TOKENS, HQ * HEAD_SIZE)
    new_values = jnp.dot(attention_rows.reshape(RESPONSE_SLOTS * SLOT_TOKENS, HQ * HEAD_SIZE), score_weight,
                         preferred_element_type=jnp.float32).reshape(RESPONSE_SLOTS, SLOT_TOKENS)
    position = jnp.arange(SLOT_TOKENS)
    live_rows = position[None, :] < lengths[:, None]
    score_delta = jnp.where(live_rows, new_values - old_values, 0.0)
    target_slot = (target_rank * SEQ_DEV + jnp.arange(RESPONSE_SLOTS) % SEQ_DEV).astype(jnp.int32)
    placed = jnp.zeros_like(attention_rows).at[target_slot].set(attention_rows)
    return placed, score_delta
```

```python
import functools
import math

import jax
import jax.numpy as jnp
from jax import lax
from jax.experimental import pallas as pl
from jax.experimental.pallas import tpu as pltpu
from jax.sharding import PartitionSpec as P

HEAD = 128
BLOCK = 16
STACK = 4
MESH = pl.DeviceIdType.MESH
NEG = -1e30


def xor(a, b, n):
    total, bit = 0, 1
    while bit < n:
        total = total + ((a // bit + b // bit) % 2) * bit
        bit *= 2
    return total


def score_kernel(
    n, rows, slot_len,
    order_ref, lo_ref, hi_ref, tok_ref, q_ref, kv_ref, prompt_ref, w_ref, old_ref,
    recv_ref, delta_ref,
    keys, vals, qf, kvf, qc, send, nv_send, nv_recv,
    send_sem, recv_sem, self_sem, nv_send_sem, nv_recv_sem,
):
    me = lax.axis_index("dp")
    core = lax.axis_index("tensor")
    slots = q_ref.shape[0]
    blocks = slots // BLOCK
    per_block = n // blocks
    part = rows // per_block
    tokens = BLOCK * slot_len
    prompt_len = prompt_ref.shape[0]
    pair_heads = prompt_ref.shape[1] // (2 * HEAD)
    groups = q_ref.shape[2] // HEAD // pair_heads
    scale = HEAD ** -0.5 * math.log2(math.e)

    barrier = pltpu.get_barrier_semaphore()

    def greet(m, _):
        pl.semaphore_signal(
            barrier, inc=1, device_id={"dp": xor(me, m, n)}, device_id_type=MESH
        )
        return _

    lax.fori_loop(1, n, greet, 0)
    pl.semaphore_signal(barrier, inc=1, device_id={"tensor": 1 - core}, device_id_type=MESH)

    def put_keys(g, at, size, k, v):
        scaled = k.astype(jnp.float32) * scale
        high = scaled.astype(jnp.bfloat16)
        low = (scaled - high.astype(jnp.float32)).astype(jnp.bfloat16)
        keys[g, pl.ds(at, size), :HEAD] = high
        keys[g, pl.ds(at, size), HEAD:] = low
        vals[g, pl.ds(at, size), :HEAD] = v

    vals[:, :, HEAD:] = jnp.ones_like(vals[:, :, HEAD:])
    for g in range(pair_heads):
        col = g * 2 * HEAD
        put_keys(g, 0, prompt_len, prompt_ref[:, col : col + HEAD],
                 prompt_ref[:, col + HEAD : col + 2 * HEAD])
    nv_send[...] = jnp.zeros_like(nv_send)
    pl.semaphore_wait(barrier, n)

    def outgoing(k):
        block, g = k // per_block, k % per_block
        return pltpu.make_async_remote_copy(
            src_ref=send.at[block, pl.ds(g * part, part)],
            dst_ref=recv_ref.at[k],
            send_sem=send_sem.at[k],
            recv_sem=recv_sem.at[k],
            device_id={"dp": xor(me, n - 1 - k, n)},
            device_id_type=MESH,
        )

    def one_block(j, _):
        for i in range(BLOCK):
            slot = order_ref[j * BLOCK + i]
            qf[pl.ds(i * slot_len, slot_len), :] = q_ref[slot].astype(jnp.float32)
            kvf[pl.ds(i * slot_len, slot_len), :] = kv_ref[slot].astype(jnp.float32)
        row = lax.broadcasted_iota(jnp.int32, (rows, tokens), 0)
        lo, hi = lo_ref[j], hi_ref[j]
        pick = jnp.where((lo == row) & (lo < hi), 1.0, 0.0).astype(jnp.bfloat16)
        qc[...] = jnp.dot(
            pick, qf[...].astype(jnp.bfloat16), preferred_element_type=jnp.float32
        ).astype(jnp.bfloat16)
        bias = jnp.where((lo <= row) & (row < hi), 0.0, NEG)
        bias = jnp.concatenate([bias] * STACK, axis=0)
        for g in range(pair_heads):
            col = g * 2 * HEAD
            put_keys(g, prompt_len, tokens, kvf[:, col : col + HEAD],
                     kvf[:, col + HEAD : col + 2 * HEAD].astype(jnp.bfloat16))

        def heads(step, nv):
            g = step // (groups // STACK)
            base = step * STACK * HEAD
            cols = [pl.ds(pl.multiple_of(base + h * HEAD, HEAD), HEAD) for h in range(STACK)]
            q = jnp.concatenate([qc[:, c] for c in cols], axis=0)
            q = jnp.concatenate([q, q], axis=1)
            s = lax.dot_general(
                q, keys[g], (((1,), (1,)), ((), ())), preferred_element_type=jnp.float32
            )
            sp = s[:, :prompt_len]
            so = s[:, prompt_len:] + bias
            top = jnp.maximum(
                jnp.max(sp, axis=1, keepdims=True), jnp.max(so, axis=1, keepdims=True)
            )
            probs = jnp.concatenate(
                [jnp.exp2(sp - top).astype(jnp.bfloat16), jnp.exp2(so - top).astype(jnp.bfloat16)],
                axis=1,
            )
            o = jnp.dot(probs, vals[g], preferred_element_type=jnp.float32)
            r = (o[:, :HEAD] / o[:, HEAD:]).astype(jnp.bfloat16)
            for h, c in enumerate(cols):
                piece = r[h * rows : (h + 1) * rows]
                send[j, :, c] = piece
                nv = nv + piece.astype(jnp.float32) * w_ref[:, c].astype(jnp.float32)
            return nv

        nv = lax.fori_loop(
            0, pair_heads * groups // STACK, heads, jnp.zeros((rows, HEAD), jnp.float32)
        )
        nv = jnp.sum(nv, axis=1, keepdims=True)
        wide = lax.broadcasted_iota(jnp.int32, (rows, slots * slot_len), 0) + j * rows
        nv_send[...] += jnp.sum(jnp.where(tok_ref[...] == wide, nv, 0.0), axis=0, keepdims=True)

        def start(g, _):
            outgoing(j * per_block + g).start()
            return _

        lax.fori_loop(0, jnp.where(j == blocks - 1, per_block - 1, per_block), start, 0)
        return _

    lax.fori_loop(0, blocks, one_block, 0)

    own = pltpu.make_async_copy(
        send.at[blocks - 1, pl.ds((per_block - 1) * part, part)], recv_ref.at[n - 1], self_sem
    )
    own.start()
    trade = pltpu.make_async_remote_copy(
        src_ref=nv_send, dst_ref=nv_recv, send_sem=nv_send_sem, recv_sem=nv_recv_sem,
        device_id={"tensor": 1 - core}, device_id_type=MESH,
    )
    trade.start()
    trade.wait()
    delta_ref[...] = jnp.where(
        tok_ref[...] >= 0, nv_send[...] + nv_recv[...] - old_ref[...], 0.0
    )
    own.wait()

    def finish(k, _):
        outgoing(k).wait()
        return _

    lax.fori_loop(0, n - 1, finish, 0)


def place_kernel(rows, slot_len, order_ref, lo_ref, hi_ref, recv_ref, out_ref):
    tokens = BLOCK * slot_len
    blocks = out_ref.shape[0] // BLOCK

    def one_block(j, _):
        row = lax.broadcasted_iota(jnp.int32, (rows, tokens), 0)
        lo, hi = lo_ref[j], hi_ref[j]
        pick = jnp.where((lo == row) & (lo < hi), 1.0, 0.0).astype(jnp.bfloat16)
        full = lax.dot_general(
            pick, recv_ref[j], (((0,), (0,)), ((), ())), preferred_element_type=jnp.float32
        )
        for i in range(BLOCK):
            out_ref[order_ref[j * BLOCK + i]] = full[
                i * slot_len : (i + 1) * slot_len
            ].astype(jnp.bfloat16)
        return _

    lax.fori_loop(0, blocks, one_block, 0)


def plan(partner, lens, me, n, rows, slot_len):
    slots = lens.shape[0]
    cap = slots // n
    per_block = BLOCK // cap
    slot = jnp.arange(slots, dtype=jnp.int32)
    earlier = (partner[:, None] == partner[None, :]) & (slot[None, :] < slot[:, None])
    rank = jnp.sum(earlier.astype(jnp.int32), axis=1)
    before = jnp.sum(jnp.where(earlier, lens[None, :], 0), axis=1)
    k = n - 1 - (partner ^ me)
    at = k * cap + rank
    first = (k % per_block) * (rows // per_block) + before
    match = at[None, :] == slot[:, None]

    def sort(x):
        return jnp.sum(jnp.where(match, x[None, :], 0), axis=1)

    position = jnp.arange(slot_len, dtype=jnp.int32)
    start = sort(first)
    lo = start[:, None] + position[None, :]
    hi = jnp.broadcast_to((start + sort(lens))[:, None], lo.shape)
    shape = (slots // BLOCK, 1, BLOCK * slot_len)
    token = jnp.where(
        position[None, :] < lens[:, None],
        ((k // per_block) * rows + first)[:, None] + position[None, :],
        -1,
    )
    return sort(slot), lo.reshape(shape), hi.reshape(shape), token.reshape(1, slots * slot_len)


def shards(queries, key_value_pairs, prompt_cache, score_weight, old_values, lengths, target_rank):
    me = lax.axis_index("dp").astype(jnp.int32)
    n = lax.axis_size("dp")
    slots, slot_len, width = queries.shape
    pair_heads = prompt_cache.shape[1] // (2 * HEAD)
    prompt_len = prompt_cache.shape[0]
    blocks = slots // BLOCK
    tokens = BLOCK * slot_len
    rows = tokens
    targets = target_rank.reshape(n, slots)
    lens = lengths.reshape(n, slots)
    my_targets = lax.dynamic_index_in_dim(targets, me, 0, keepdims=False)
    my_lens = lax.dynamic_index_in_dim(lens, me, 0, keepdims=False)
    arriving = targets == me
    ranks = jnp.arange(n, dtype=jnp.int32)
    source = jnp.sum(jnp.where(arriving, ranks[:, None], 0), axis=0)
    source_lens = jnp.sum(jnp.where(arriving, lens, 0), axis=0)
    order, lo, hi, token = plan(my_targets, my_lens, me, n, rows, slot_len)
    in_order, in_lo, in_hi, _ = plan(source, source_lens, me, n, rows, slot_len)

    smem = pl.BlockSpec(memory_space=pltpu.SMEM)
    vmem = pl.BlockSpec(memory_space=pltpu.VMEM)
    part = rows * blocks // n
    recv, delta = pl.pallas_call(
        functools.partial(score_kernel, n, rows, slot_len),
        out_shape=(
            jax.ShapeDtypeStruct((n, part, width), jnp.bfloat16),
            jax.ShapeDtypeStruct((1, slots * slot_len), jnp.float32),
        ),
        in_specs=[smem] + [vmem] * 8,
        out_specs=(pl.BlockSpec(memory_space=pl.ANY), vmem),
        scratch_shapes=[
            pltpu.VMEM((pair_heads, prompt_len + tokens, 2 * HEAD), jnp.bfloat16),
            pltpu.VMEM((pair_heads, prompt_len + tokens, 2 * HEAD), jnp.bfloat16),
            pltpu.VMEM((tokens, width), jnp.float32),
            pltpu.VMEM((tokens, prompt_cache.shape[1]), jnp.float32),
            pltpu.VMEM((rows, width), jnp.bfloat16),
            pltpu.VMEM((blocks, rows, width), jnp.bfloat16),
            pltpu.VMEM((1, slots * slot_len), jnp.float32),
            pltpu.VMEM((1, slots * slot_len), jnp.float32),
            pltpu.SemaphoreType.DMA((n,)),
            pltpu.SemaphoreType.DMA((n,)),
            pltpu.SemaphoreType.DMA,
            pltpu.SemaphoreType.DMA,
            pltpu.SemaphoreType.DMA,
        ],
        compiler_params=pltpu.CompilerParams(
            collective_id=0, has_side_effects=True, vmem_limit_bytes=48 * 2**20
        ),
    )(order, lo, hi, token, queries, key_value_pairs, prompt_cache,
      score_weight.reshape(1, width), old_values.reshape(1, slots * slot_len))

    attention = pl.pallas_call(
        functools.partial(place_kernel, rows, slot_len),
        out_shape=jax.ShapeDtypeStruct((slots, slot_len, width), jnp.bfloat16),
        in_specs=[smem, vmem, vmem, vmem],
        out_specs=vmem,
        compiler_params=pltpu.CompilerParams(vmem_limit_bytes=48 * 2**20),
    )(in_order, in_lo, in_hi, recv.reshape(blocks, rows, width))
    return attention, delta.reshape(slots, slot_len)


def solution(mesh):
    placed = (
        P(("group", "dp"), None, "tensor"),
        P(("group", "dp"), None, "tensor"),
        P("group", "tensor"),
        P("tensor"),
        P(("group", "dp"), None),
        P("group"),
        P("group"),
    )
    return jax.shard_map(
        shards,
        mesh=mesh,
        in_specs=placed,
        out_specs=(P(("group", "dp"), None, "tensor"), P(("group", "dp"), None)),
        check_vma=False,
    )
```

```python
import functools
import math

import jax
import jax.numpy as jnp
from jax import lax
from jax.experimental import pallas as pl
from jax.experimental.pallas import tpu as pltpu
from jax.sharding import PartitionSpec as P

HEAD = 128
BLOCK = 16
SIZES = (80, 96)
MESH = pl.DeviceIdType.MESH
NEG = -1e30


def xor(a, b, n):
    total, bit = 0, 1
    while bit < n:
        total = total + ((a // bit + b // bit) % 2) * bit
        bit *= 2
    return total


def score_kernel(
    n, rows, slot_len,
    order_ref, lo_ref, hi_ref, tok_ref, q_ref, kv_ref, prompt_ref, w_ref, old_ref,
    recv_ref, delta_ref,
    keys, vals, qf, kvf, qc, send, nv_send, nv_recv,
    send_sem, recv_sem, self_sem, nv_send_sem, nv_recv_sem,
):
    me = lax.axis_index("dp")
    core = lax.axis_index("tensor")
    slots = q_ref.shape[0]
    blocks = slots // BLOCK
    per_block = n // blocks
    part = rows // per_block
    tokens = BLOCK * slot_len
    prompt_len = prompt_ref.shape[0]
    pair_heads = prompt_ref.shape[1] // (2 * HEAD)
    groups = q_ref.shape[2] // HEAD // pair_heads
    scale = HEAD ** -0.5 * math.log2(math.e)

    barrier = pltpu.get_barrier_semaphore()

    def greet(m, _):
        pl.semaphore_signal(
            barrier, inc=1, device_id={"dp": xor(me, m, n)}, device_id_type=MESH
        )
        return _

    lax.fori_loop(1, n, greet, 0)
    pl.semaphore_signal(barrier, inc=1, device_id={"tensor": 1 - core}, device_id_type=MESH)

    def put_keys(g, at, size, k, v):
        scaled = k.astype(jnp.float32) * scale
        high = scaled.astype(jnp.bfloat16)
        low = (scaled - high.astype(jnp.float32)).astype(jnp.bfloat16)
        keys[g, pl.ds(at, size), :HEAD] = high
        keys[g, pl.ds(at, size), HEAD:] = low
        vals[g, pl.ds(at, size), :HEAD] = v

    vals[:, :, HEAD:] = jnp.ones_like(vals[:, :, HEAD:])
    for g in range(pair_heads):
        col = g * 2 * HEAD
        put_keys(g, 0, prompt_len, prompt_ref[:, col : col + HEAD],
                 prompt_ref[:, col + HEAD : col + 2 * HEAD])
    nv_send[...] = jnp.zeros_like(nv_send)
    pl.semaphore_wait(barrier, n)

    def outgoing(k, g):
        block, at = k // per_block, k % per_block
        return pltpu.make_async_remote_copy(
            src_ref=send.at[block, g, pl.ds(at * part, part)],
            dst_ref=recv_ref.at[block, g, pl.ds(at * part, part)],
            send_sem=send_sem.at[k, g],
            recv_sem=recv_sem.at[k, g],
            device_id={"dp": xor(me, n - 1 - k, n)},
            device_id_type=MESH,
        )

    def one_block(j, _):
        for i in range(BLOCK):
            slot = order_ref[j * BLOCK + i]
            qf[pl.ds(i * slot_len, slot_len), :] = q_ref[slot].astype(jnp.float32)
            kvf[pl.ds(i * slot_len, slot_len), :] = kv_ref[slot].astype(jnp.float32)
        row = lax.broadcasted_iota(jnp.int32, (rows, tokens), 0)
        lo, hi = lo_ref[j], hi_ref[j]
        pick = jnp.where((lo == row) & (lo < hi), 1.0, 0.0).astype(jnp.bfloat16)
        qc[...] = jnp.dot(
            pick, qf[...].astype(jnp.bfloat16), preferred_element_type=jnp.float32
        ).astype(jnp.bfloat16)
        bias = jnp.where((lo <= row) & (row < hi), 0.0, NEG)
        bias = jnp.concatenate([bias] * groups, axis=0)
        for g in range(pair_heads):
            col = g * 2 * HEAD
            put_keys(g, prompt_len, tokens, kvf[:, col : col + HEAD],
                     kvf[:, col + HEAD : col + 2 * HEAD].astype(jnp.bfloat16))

        def heads(g, nv):
            base = g * groups * HEAD
            cols = [pl.ds(pl.multiple_of(base + h * HEAD, HEAD), HEAD) for h in range(groups)]
            q = jnp.concatenate([qc[:, c] for c in cols], axis=0)
            q = jnp.concatenate([q, q], axis=1)
            s = lax.dot_general(
                q, keys[g], (((1,), (1,)), ((), ())), preferred_element_type=jnp.float32
            )
            sp = s[:, :prompt_len]
            so = s[:, prompt_len:] + bias
            top = jnp.maximum(
                jnp.max(sp, axis=1, keepdims=True), jnp.max(so, axis=1, keepdims=True)
            )
            probs = jnp.concatenate(
                [jnp.exp2(sp - top).astype(jnp.bfloat16), jnp.exp2(so - top).astype(jnp.bfloat16)],
                axis=1,
            )
            o = jnp.dot(probs, vals[g], preferred_element_type=jnp.float32)
            r = (o[:, :HEAD] / o[:, HEAD:]).astype(jnp.bfloat16)
            for h, c in enumerate(cols):
                piece = r[h * rows : (h + 1) * rows]
                send[j, g, :, h * HEAD : (h + 1) * HEAD] = piece
                nv = nv + piece.astype(jnp.float32) * w_ref[:, c].astype(jnp.float32)

            def start(at, _):
                outgoing(j * per_block + at, g).start()
                return _

            lax.fori_loop(0, jnp.where(j == blocks - 1, per_block - 1, per_block), start, 0)
            return nv

        nv = lax.fori_loop(0, pair_heads, heads, jnp.zeros((rows, HEAD), jnp.float32))
        nv = jnp.sum(nv, axis=1, keepdims=True)
        wide = lax.broadcasted_iota(jnp.int32, (rows, slots * slot_len), 0) + j * tokens
        nv_send[...] += jnp.sum(jnp.where(tok_ref[...] == wide, nv, 0.0), axis=0, keepdims=True)
        return _

    lax.fori_loop(0, blocks, one_block, 0)

    own = pltpu.make_async_copy(
        send.at[blocks - 1, :, pl.ds((per_block - 1) * part, part)],
        recv_ref.at[blocks - 1, :, pl.ds((per_block - 1) * part, part)],
        self_sem,
    )
    own.start()
    trade = pltpu.make_async_remote_copy(
        src_ref=nv_send, dst_ref=nv_recv, send_sem=nv_send_sem, recv_sem=nv_recv_sem,
        device_id={"tensor": 1 - core}, device_id_type=MESH,
    )
    trade.start()
    trade.wait()
    delta_ref[...] = jnp.where(
        tok_ref[...] >= 0, nv_send[...] + nv_recv[...] - old_ref[...], 0.0
    )
    own.wait()

    def finish(k, _):
        for g in range(pair_heads):
            outgoing(k, g).wait()
        return _

    lax.fori_loop(0, n - 1, finish, 0)


def place_kernel(rows, slot_len, order_ref, lo_ref, hi_ref, recv_ref, out_ref):
    tokens = BLOCK * slot_len
    blocks = out_ref.shape[0] // BLOCK

    def one_block(j, _):
        row = lax.broadcasted_iota(jnp.int32, (rows, tokens), 0)
        lo, hi = lo_ref[j], hi_ref[j]
        pick = jnp.where((lo == row) & (lo < hi), 1.0, 0.0).astype(jnp.bfloat16)
        half = recv_ref.shape[3]
        for g in range(recv_ref.shape[1]):
            full = lax.dot_general(
                pick, recv_ref[j, g], (((0,), (0,)), ((), ())), preferred_element_type=jnp.float32
            )
            for i in range(BLOCK):
                out_ref[order_ref[j * BLOCK + i], :, g * half : (g + 1) * half] = full[
                    i * slot_len : (i + 1) * slot_len
                ].astype(jnp.bfloat16)
        return _

    lax.fori_loop(0, blocks, one_block, 0)


def plan(partner, lens, me, n, rows, slot_len):
    slots = lens.shape[0]
    cap = slots // n
    per_block = BLOCK // cap
    slot = jnp.arange(slots, dtype=jnp.int32)
    earlier = (partner[:, None] == partner[None, :]) & (slot[None, :] < slot[:, None])
    rank = jnp.sum(earlier.astype(jnp.int32), axis=1)
    before = jnp.sum(jnp.where(earlier, lens[None, :], 0), axis=1)
    k = n - 1 - (partner ^ me)
    at = k * cap + rank
    first = (k % per_block) * (rows // per_block) + before
    match = at[None, :] == slot[:, None]

    def sort(x):
        return jnp.sum(jnp.where(match, x[None, :], 0), axis=1)

    position = jnp.arange(slot_len, dtype=jnp.int32)
    start = sort(first)
    lo = start[:, None] + position[None, :]
    hi = jnp.broadcast_to((start + sort(lens))[:, None], lo.shape)
    shape = (slots // BLOCK, 1, BLOCK * slot_len)
    token = jnp.where(
        position[None, :] < lens[:, None],
        ((k // per_block) * (BLOCK * slot_len) + first)[:, None] + position[None, :],
        -1,
    )
    return sort(slot), lo.reshape(shape), hi.reshape(shape), token.reshape(1, slots * slot_len)


def shards(queries, key_value_pairs, prompt_cache, score_weight, old_values, lengths, target_rank):
    me = lax.axis_index("dp").astype(jnp.int32)
    n = lax.axis_size("dp")
    slots, slot_len, width = queries.shape
    pair_heads = prompt_cache.shape[1] // (2 * HEAD)
    prompt_len = prompt_cache.shape[0]
    blocks = slots // BLOCK
    tokens = BLOCK * slot_len
    targets = target_rank.reshape(n, slots)
    lens = lengths.reshape(n, slots)
    my_targets = lax.dynamic_index_in_dim(targets, me, 0, keepdims=False)
    my_lens = lax.dynamic_index_in_dim(lens, me, 0, keepdims=False)
    arriving = targets == me
    ranks = jnp.arange(n, dtype=jnp.int32)
    source = jnp.sum(jnp.where(arriving, ranks[:, None], 0), axis=0)
    source_lens = jnp.sum(jnp.where(arriving, lens, 0), axis=0)
    order, lo, hi, token = plan(my_targets, my_lens, me, n, tokens, slot_len)
    in_order, in_lo, in_hi, _ = plan(source, source_lens, me, n, tokens, slot_len)

    smem = pl.BlockSpec(memory_space=pltpu.SMEM)
    vmem = pl.BlockSpec(memory_space=pltpu.VMEM)

    def attend(rows, call_id, operands, arrivals):
        half = width // pair_heads
        parcels = (blocks, pair_heads, rows, half)
        recv, delta = pl.pallas_call(
            functools.partial(score_kernel, n, rows, slot_len),
            out_shape=(
                jax.ShapeDtypeStruct(parcels, jnp.bfloat16),
                jax.ShapeDtypeStruct((1, slots * slot_len), jnp.float32),
            ),
            in_specs=[smem] + [vmem] * 8,
            out_specs=(pl.BlockSpec(memory_space=pl.ANY), vmem),
            scratch_shapes=[
                pltpu.VMEM((pair_heads, prompt_len + tokens, 2 * HEAD), jnp.bfloat16),
                pltpu.VMEM((pair_heads, prompt_len + tokens, 2 * HEAD), jnp.bfloat16),
                pltpu.VMEM((tokens, width), jnp.float32),
                pltpu.VMEM((tokens, prompt_cache.shape[1]), jnp.float32),
                pltpu.VMEM((rows, width), jnp.bfloat16),
                pltpu.VMEM(parcels, jnp.bfloat16),
                pltpu.VMEM((1, slots * slot_len), jnp.float32),
                pltpu.VMEM((1, slots * slot_len), jnp.float32),
                pltpu.SemaphoreType.DMA((n, pair_heads)),
                pltpu.SemaphoreType.DMA((n, pair_heads)),
                pltpu.SemaphoreType.DMA,
                pltpu.SemaphoreType.DMA,
                pltpu.SemaphoreType.DMA,
            ],
            compiler_params=pltpu.CompilerParams(
                collective_id=call_id, has_side_effects=True, vmem_limit_bytes=48 * 2**20
            ),
        )(*operands)
        attention = pl.pallas_call(
            functools.partial(place_kernel, rows, slot_len),
            out_shape=jax.ShapeDtypeStruct((slots, slot_len, width), jnp.bfloat16),
            in_specs=[smem, vmem, vmem, vmem],
            out_specs=vmem,
            compiler_params=pltpu.CompilerParams(vmem_limit_bytes=48 * 2**20),
        )(*arrivals, recv)
        return attention, delta

    operands = (order, lo, hi, token, queries, key_value_pairs, prompt_cache,
                score_weight.reshape(1, width), old_values.reshape(1, slots * slot_len))
    arrivals = (in_order, in_lo, in_hi)
    if n == blocks:
        pair = targets[:, None, :] == ranks[None, :, None]
        most = jnp.max(jnp.sum(jnp.where(pair, lens[:, None, :], 0), axis=2))
        most = lax.pmax(most.reshape(1), "group")[0]
        sizes = [size for size in SIZES if size < tokens] + [tokens]
        choice = sum((most > size).astype(jnp.int32) for size in sizes[:-1])
        branches = [functools.partial(attend, size, i) for i, size in enumerate(sizes)]
        attention, delta = lax.switch(choice, branches, operands, arrivals)
    else:
        attention, delta = attend(tokens, 0, operands, arrivals)
    return attention, delta.reshape(slots, slot_len)


def solution(mesh):
    placed = (
        P(("group", "dp"), None, "tensor"),
        P(("group", "dp"), None, "tensor"),
        P("group", "tensor"),
        P("tensor"),
        P(("group", "dp"), None),
        P("group"),
        P("group"),
    )
    return jax.shard_map(
        shards,
        mesh=mesh,
        in_specs=placed,
        out_specs=(P(("group", "dp"), None, "tensor"), P(("group", "dp"), None)),
        check_vma=False,
    )
```

```python
import functools
import math

import jax
import jax.numpy as jnp
from jax import lax
from jax.experimental import pallas as pl
from jax.experimental.pallas import tpu as pltpu
from jax.sharding import PartitionSpec as P

HEAD = 128
BLOCK = 16
COLUMNS = 512
SIZES = (80, 96)
MESH = pl.DeviceIdType.MESH
NEG = -1e30


def xor(a, b, n):
    total, bit = 0, 1
    while bit < n:
        total = total + ((a // bit + b // bit) % 2) * bit
        bit *= 2
    return total


def score_kernel(
    n, rows, slot_len,
    order_ref, lo_ref, hi_ref, tok_ref, q_ref, kv_ref, prompt_ref, w_ref, old_ref,
    recv_ref, delta_ref,
    keys, vals, qf, kvf, qc, send, nv_send, nv_recv,
    send_sem, recv_sem, self_sem, nv_send_sem, nv_recv_sem,
):
    me = lax.axis_index("dp")
    core = lax.axis_index("tensor")
    slots = q_ref.shape[0]
    blocks = slots // BLOCK
    per_block = n // blocks
    part = rows // per_block
    tokens = BLOCK * slot_len
    prompt_len = prompt_ref.shape[0]
    pair_heads = prompt_ref.shape[1] // (2 * HEAD)
    groups = q_ref.shape[2] // HEAD // pair_heads
    scale = HEAD ** -0.5 * math.log2(math.e)

    barrier = pltpu.get_barrier_semaphore()

    def greet(m, _):
        pl.semaphore_signal(
            barrier, inc=1, device_id={"dp": xor(me, m, n)}, device_id_type=MESH
        )
        return _

    lax.fori_loop(1, n, greet, 0)
    pl.semaphore_signal(barrier, inc=1, device_id={"tensor": 1 - core}, device_id_type=MESH)

    def put_keys(g, at, size, k, v):
        scaled = k.astype(jnp.float32) * scale
        high = scaled.astype(jnp.bfloat16)
        low = (scaled - high.astype(jnp.float32)).astype(jnp.bfloat16)
        keys[g, pl.ds(at, size), :HEAD] = high
        keys[g, pl.ds(at, size), HEAD:] = low
        vals[g, pl.ds(at, size), :HEAD] = v

    vals[:, :, HEAD:] = jnp.ones_like(vals[:, :, HEAD:])
    for g in range(pair_heads):
        col = g * 2 * HEAD
        put_keys(g, 0, prompt_len, prompt_ref[:, col : col + HEAD],
                 prompt_ref[:, col + HEAD : col + 2 * HEAD])
    nv_send[...] = jnp.zeros_like(nv_send)
    pl.semaphore_wait(barrier, n)

    def outgoing(k, g):
        block, at = k // per_block, k % per_block
        return pltpu.make_async_remote_copy(
            src_ref=send.at[block, g, pl.ds(at * part, part)],
            dst_ref=recv_ref.at[block, g, pl.ds(at * part, part)],
            send_sem=send_sem.at[k, g],
            recv_sem=recv_sem.at[k, g],
            device_id={"dp": xor(me, n - 1 - k, n)},
            device_id_type=MESH,
        )

    def one_block(j, _):
        for i in range(BLOCK):
            slot = order_ref[j * BLOCK + i]
            qf[pl.ds(i * slot_len, slot_len), :] = q_ref[slot].astype(jnp.float32)
            kvf[pl.ds(i * slot_len, slot_len), :] = kv_ref[slot].astype(jnp.float32)
        row = lax.broadcasted_iota(jnp.int32, (rows, tokens), 0)
        lo, hi = lo_ref[j], hi_ref[j]
        pick = jnp.where((lo == row) & (lo < hi), 1.0, 0.0).astype(jnp.bfloat16)
        qc[...] = jnp.dot(
            pick, qf[...].astype(jnp.bfloat16), preferred_element_type=jnp.float32
        ).astype(jnp.bfloat16)
        bias = jnp.where((lo <= row) & (row < hi), 0.0, NEG)
        bias = jnp.concatenate([bias] * groups, axis=0)
        for g in range(pair_heads):
            col = g * 2 * HEAD
            put_keys(g, prompt_len, tokens, kvf[:, col : col + HEAD],
                     kvf[:, col + HEAD : col + 2 * HEAD].astype(jnp.bfloat16))

        def heads(g, nv):
            base = g * groups * HEAD
            cols = [pl.ds(pl.multiple_of(base + h * HEAD, HEAD), HEAD) for h in range(groups)]
            q = jnp.concatenate([qc[:, c] for c in cols], axis=0)
            q = jnp.concatenate([q, q], axis=1)
            s = lax.dot_general(
                q, keys[g], (((1,), (1,)), ((), ())), preferred_element_type=jnp.float32
            )
            sp = s[:, :prompt_len]
            so = s[:, prompt_len:] + bias
            top = jnp.maximum(
                jnp.max(sp, axis=1, keepdims=True), jnp.max(so, axis=1, keepdims=True)
            )
            probs = jnp.concatenate(
                [jnp.exp2(sp - top).astype(jnp.bfloat16), jnp.exp2(so - top).astype(jnp.bfloat16)],
                axis=1,
            )
            o = jnp.dot(probs, vals[g], preferred_element_type=jnp.float32)
            r = (o[:, :HEAD] / o[:, HEAD:]).astype(jnp.bfloat16)
            for h, c in enumerate(cols):
                piece = r[h * rows : (h + 1) * rows]
                send[j, g, :, h * HEAD : (h + 1) * HEAD] = piece
                nv = nv + piece.astype(jnp.float32) * w_ref[:, c].astype(jnp.float32)

            def start(at, _):
                outgoing(j * per_block + at, g).start()
                return _

            lax.fori_loop(0, jnp.where(j == blocks - 1, per_block - 1, per_block), start, 0)
            return nv

        nv = lax.fori_loop(0, pair_heads, heads, jnp.zeros((rows, HEAD), jnp.float32))
        nv = jnp.sum(nv, axis=1, keepdims=True)
        wide = lax.broadcasted_iota(jnp.int32, (rows, slots * slot_len), 0) + j * tokens
        nv_send[...] += jnp.sum(jnp.where(tok_ref[...] == wide, nv, 0.0), axis=0, keepdims=True)
        return _

    lax.fori_loop(0, blocks, one_block, 0)

    own = pltpu.make_async_copy(
        send.at[blocks - 1, :, pl.ds((per_block - 1) * part, part)],
        recv_ref.at[blocks - 1, :, pl.ds((per_block - 1) * part, part)],
        self_sem,
    )
    own.start()
    trade = pltpu.make_async_remote_copy(
        src_ref=nv_send, dst_ref=nv_recv, send_sem=nv_send_sem, recv_sem=nv_recv_sem,
        device_id={"tensor": 1 - core}, device_id_type=MESH,
    )
    trade.start()
    trade.wait()
    wide = (slots, slots * slot_len)
    mine = lax.broadcasted_iota(jnp.int32, wide, 1) // slot_len == lax.broadcasted_iota(
        jnp.int32, wide, 0
    )
    tall = (slots * slot_len, slot_len)
    spread = jnp.where(
        lax.broadcasted_iota(jnp.int32, tall, 0) % slot_len
        == lax.broadcasted_iota(jnp.int32, tall, 1),
        1.0,
        0.0,
    )

    def fold(x):
        return jnp.dot(
            jnp.where(mine, x, 0.0), spread,
            precision=lax.Precision.HIGHEST, preferred_element_type=jnp.float32,
        )

    live = fold(jnp.where(tok_ref[...] >= 0, 1.0, 0.0))
    delta_ref[...] = jnp.where(
        live > 0.5, fold(nv_send[...] + nv_recv[...]) - old_ref[...], 0.0
    )
    own.wait()

    def finish(k, _):
        for g in range(pair_heads):
            outgoing(k, g).wait()
        return _

    lax.fori_loop(0, n - 1, finish, 0)


def place_kernel(rows, slot_len, order_ref, lo_ref, hi_ref, recv_ref, out_ref):
    tokens = BLOCK * slot_len
    blocks = out_ref.shape[0] // BLOCK

    def one_block(j, _):
        row = lax.broadcasted_iota(jnp.int32, (rows, tokens), 0)
        lo, hi = lo_ref[j], hi_ref[j]
        pick = jnp.where((lo == row) & (lo < hi), 1.0, 0.0).astype(jnp.bfloat16)
        full = lax.dot_general(
            pick, recv_ref[j, 0], (((0,), (0,)), ((), ())), preferred_element_type=jnp.float32
        )
        for i in range(BLOCK):
            out_ref[order_ref[j * BLOCK + i]] = full[
                i * slot_len : (i + 1) * slot_len
            ].astype(jnp.bfloat16)
        return _

    lax.fori_loop(0, blocks, one_block, 0)


def plan(partner, lens, me, n, rows, slot_len):
    slots = lens.shape[0]
    cap = slots // n
    per_block = BLOCK // cap
    slot = jnp.arange(slots, dtype=jnp.int32)
    earlier = (partner[:, None] == partner[None, :]) & (slot[None, :] < slot[:, None])
    rank = jnp.sum(earlier.astype(jnp.int32), axis=1)
    before = jnp.sum(jnp.where(earlier, lens[None, :], 0), axis=1)
    k = n - 1 - (partner ^ me)
    at = k * cap + rank
    first = (k % per_block) * (rows // per_block) + before
    match = at[None, :] == slot[:, None]

    def sort(x):
        return jnp.sum(jnp.where(match, x[None, :], 0), axis=1)

    position = jnp.arange(slot_len, dtype=jnp.int32)
    start = sort(first)
    lo = start[:, None] + position[None, :]
    hi = jnp.broadcast_to((start + sort(lens))[:, None], lo.shape)
    shape = (slots // BLOCK, 1, BLOCK * slot_len)
    token = jnp.where(
        position[None, :] < lens[:, None],
        ((k // per_block) * (BLOCK * slot_len) + first)[:, None] + position[None, :],
        -1,
    )
    return sort(slot), lo.reshape(shape), hi.reshape(shape), token.reshape(1, slots * slot_len)


def shards(queries, key_value_pairs, prompt_cache, score_weight, old_values, lengths, target_rank):
    me = lax.axis_index("dp").astype(jnp.int32)
    n = lax.axis_size("dp")
    slots, slot_len, width = queries.shape
    pair_heads = prompt_cache.shape[1] // (2 * HEAD)
    prompt_len = prompt_cache.shape[0]
    blocks = slots // BLOCK
    tokens = BLOCK * slot_len
    targets = target_rank.reshape(n, slots)
    lens = lengths.reshape(n, slots)
    my_targets = lax.dynamic_index_in_dim(targets, me, 0, keepdims=False)
    my_lens = lax.dynamic_index_in_dim(lens, me, 0, keepdims=False)
    arriving = targets == me
    ranks = jnp.arange(n, dtype=jnp.int32)
    source = jnp.sum(jnp.where(arriving, ranks[:, None], 0), axis=0)
    source_lens = jnp.sum(jnp.where(arriving, lens, 0), axis=0)
    order, lo, hi, token = plan(my_targets, my_lens, me, n, tokens, slot_len)
    in_order, in_lo, in_hi, _ = plan(source, source_lens, me, n, tokens, slot_len)

    smem = pl.BlockSpec(memory_space=pltpu.SMEM)
    vmem = pl.BlockSpec(memory_space=pltpu.VMEM)

    def attend(rows, call_id, operands, arrivals):
        half = width // pair_heads
        parcels = (blocks, pair_heads, rows, half)
        recv, delta = pl.pallas_call(
            functools.partial(score_kernel, n, rows, slot_len),
            out_shape=(
                jax.ShapeDtypeStruct(parcels, jnp.bfloat16),
                jax.ShapeDtypeStruct((slots, slot_len), jnp.float32),
            ),
            in_specs=[smem] + [vmem] * 8,
            out_specs=(pl.BlockSpec(memory_space=pl.ANY), vmem),
            scratch_shapes=[
                pltpu.VMEM((pair_heads, prompt_len + tokens, 2 * HEAD), jnp.bfloat16),
                pltpu.VMEM((pair_heads, prompt_len + tokens, 2 * HEAD), jnp.bfloat16),
                pltpu.VMEM((tokens, width), jnp.float32),
                pltpu.VMEM((tokens, prompt_cache.shape[1]), jnp.float32),
                pltpu.VMEM((rows, width), jnp.bfloat16),
                pltpu.VMEM(parcels, jnp.bfloat16),
                pltpu.VMEM((1, slots * slot_len), jnp.float32),
                pltpu.VMEM((1, slots * slot_len), jnp.float32),
                pltpu.SemaphoreType.DMA((n, pair_heads)),
                pltpu.SemaphoreType.DMA((n, pair_heads)),
                pltpu.SemaphoreType.DMA,
                pltpu.SemaphoreType.DMA,
                pltpu.SemaphoreType.DMA,
            ],
            compiler_params=pltpu.CompilerParams(
                collective_id=call_id, has_side_effects=True, vmem_limit_bytes=48 * 2**20
            ),
        )(*operands)
        attention = pl.pallas_call(
            functools.partial(place_kernel, rows, slot_len),
            out_shape=jax.ShapeDtypeStruct((slots, slot_len, width), jnp.bfloat16),
            grid=(width // COLUMNS,),
            in_specs=[
                smem, vmem, vmem,
                pl.BlockSpec(
                    (blocks, 1, rows, COLUMNS),
                    lambda c: (0, c // (half // COLUMNS), 0, c % (half // COLUMNS)),
                ),
            ],
            out_specs=pl.BlockSpec((slots, slot_len, COLUMNS), lambda c: (0, 0, c)),
            compiler_params=pltpu.CompilerParams(vmem_limit_bytes=48 * 2**20),
        )(*arrivals, recv)
        return attention, delta

    operands = (order, lo, hi, token, queries, key_value_pairs, prompt_cache,
                score_weight.reshape(1, width), old_values)
    arrivals = (in_order, in_lo, in_hi)
    if n == blocks:
        pair = targets[:, None, :] == ranks[None, :, None]
        most = jnp.max(jnp.sum(jnp.where(pair, lens[:, None, :], 0), axis=2))
        mine, most = most.reshape(1), most.reshape(1)
        parts = lax.axis_size("group")
        for hop in range(1, parts):
            pairs = [(i, (i + hop) % parts) for i in range(parts)]
            most = jnp.maximum(most, lax.ppermute(mine, "group", pairs))
        most = most[0]
        sizes = [size for size in SIZES if size < tokens] + [tokens]
        choice = sum((most > size).astype(jnp.int32) for size in sizes[:-1])
        branches = [functools.partial(attend, size, i) for i, size in enumerate(sizes)]
        attention, delta = lax.switch(choice, branches, operands, arrivals)
    else:
        attention, delta = attend(tokens, 0, operands, arrivals)
    return attention, delta


def solution(mesh):
    placed = (
        P(("group", "dp"), None, "tensor"),
        P(("group", "dp"), None, "tensor"),
        P("group", "tensor"),
        P("tensor"),
        P(("group", "dp"), None),
        P("group"),
        P("group"),
    )
    return jax.shard_map(
        shards,
        mesh=mesh,
        in_specs=placed,
        out_specs=(P(("group", "dp"), None, "tensor"), P(("group", "dp"), None)),
        check_vma=False,
    )
```

```python
import functools
import math

import jax
import jax.numpy as jnp
from jax import lax
from jax.experimental import pallas as pl
from jax.experimental.pallas import tpu as pltpu
from jax.sharding import PartitionSpec as P

HEAD = 128
BLOCK = 16
SIZES = (80, 96)
MESH = pl.DeviceIdType.MESH
NEG = -1e30


def xor(a, b, n):
    total, bit = 0, 1
    while bit < n:
        total = total + ((a // bit + b // bit) % 2) * bit
        bit *= 2
    return total


def score_kernel(
    n, rows, slot_len,
    order_ref, lo_ref, hi_ref, tok_ref, q_ref, kv_ref, prompt_ref, w_ref, old_ref,
    recv_ref, delta_ref,
    keys, vals, qf, kvf, qc, send, nv_send, nv_recv,
    send_sem, recv_sem, self_sem, nv_send_sem, nv_recv_sem,
):
    me = lax.axis_index("dp")
    core = lax.axis_index("tensor")
    slots = q_ref.shape[0]
    blocks = slots // BLOCK
    per_block = n // blocks
    part = rows // per_block
    tokens = BLOCK * slot_len
    prompt_len = prompt_ref.shape[0]
    pair_heads = prompt_ref.shape[1] // (2 * HEAD)
    groups = q_ref.shape[2] // HEAD // pair_heads
    scale = HEAD ** -0.5 * math.log2(math.e)

    barrier = pltpu.get_barrier_semaphore()

    def greet(m, _):
        pl.semaphore_signal(
            barrier, inc=1, device_id={"dp": xor(me, m, n)}, device_id_type=MESH
        )
        return _

    lax.fori_loop(1, n, greet, 0)
    pl.semaphore_signal(barrier, inc=1, device_id={"tensor": 1 - core}, device_id_type=MESH)

    def put_keys(g, at, size, k, v):
        scaled = k.astype(jnp.float32) * scale
        high = scaled.astype(jnp.bfloat16)
        low = (scaled - high.astype(jnp.float32)).astype(jnp.bfloat16)
        keys[g, pl.ds(at, size), :HEAD] = high
        keys[g, pl.ds(at, size), HEAD:] = low
        vals[g, pl.ds(at, size), :HEAD] = v

    vals[:, :, HEAD:] = jnp.ones_like(vals[:, :, HEAD:])
    for g in range(pair_heads):
        col = g * 2 * HEAD
        put_keys(g, 0, prompt_len, prompt_ref[:, col : col + HEAD],
                 prompt_ref[:, col + HEAD : col + 2 * HEAD])
    nv_send[...] = jnp.zeros_like(nv_send)
    pl.semaphore_wait(barrier, n)

    def outgoing(k, g):
        block, at = k // per_block, k % per_block
        return pltpu.make_async_remote_copy(
            src_ref=send.at[block, g, pl.ds(at * part, part)],
            dst_ref=recv_ref.at[block, g, pl.ds(at * part, part)],
            send_sem=send_sem.at[k, g],
            recv_sem=recv_sem.at[k, g],
            device_id={"dp": xor(me, n - 1 - k, n)},
            device_id_type=MESH,
        )

    def one_block(j, _):
        for i in range(BLOCK):
            slot = order_ref[j * BLOCK + i]
            qf[pl.ds(i * slot_len, slot_len), :] = q_ref[slot].astype(jnp.float32)
            kvf[pl.ds(i * slot_len, slot_len), :] = kv_ref[slot].astype(jnp.float32)
        row = lax.broadcasted_iota(jnp.int32, (rows, tokens), 0)
        lo, hi = lo_ref[j], hi_ref[j]
        pick = jnp.where((lo == row) & (lo < hi), 1.0, 0.0).astype(jnp.bfloat16)
        qc[...] = jnp.dot(
            pick, qf[...].astype(jnp.bfloat16), preferred_element_type=jnp.float32
        ).astype(jnp.bfloat16)
        bias = jnp.where((lo <= row) & (row < hi), 0.0, NEG)
        bias = jnp.concatenate([bias] * groups, axis=0)
        for g in range(pair_heads):
            col = g * 2 * HEAD
            put_keys(g, prompt_len, tokens, kvf[:, col : col + HEAD],
                     kvf[:, col + HEAD : col + 2 * HEAD].astype(jnp.bfloat16))

        def heads(g, nv):
            base = g * groups * HEAD
            cols = [pl.ds(pl.multiple_of(base + h * HEAD, HEAD), HEAD) for h in range(groups)]
            q = jnp.concatenate([qc[:, c] for c in cols], axis=0)
            q = jnp.concatenate([q, q], axis=1)
            s = lax.dot_general(
                q, keys[g], (((1,), (1,)), ((), ())), preferred_element_type=jnp.float32
            )
            sp = s[:, :prompt_len]
            so = s[:, prompt_len:] + bias
            top = jnp.maximum(
                jnp.max(sp, axis=1, keepdims=True), jnp.max(so, axis=1, keepdims=True)
            )
            probs = jnp.concatenate(
                [jnp.exp2(sp - top).astype(jnp.bfloat16), jnp.exp2(so - top).astype(jnp.bfloat16)],
                axis=1,
            )
            o = jnp.dot(probs, vals[g], preferred_element_type=jnp.float32)
            r = (o[:, :HEAD] / o[:, HEAD:]).astype(jnp.bfloat16)
            for h, c in enumerate(cols):
                piece = r[h * rows : (h + 1) * rows]
                send[j, g, :, h * HEAD : (h + 1) * HEAD] = piece
                nv = nv + piece.astype(jnp.float32) * w_ref[:, c].astype(jnp.float32)

            def start(at, _):
                outgoing(j * per_block + at, g).start()
                return _

            lax.fori_loop(0, jnp.where(j == blocks - 1, per_block - 1, per_block), start, 0)
            return nv

        nv = lax.fori_loop(0, pair_heads, heads, jnp.zeros((rows, HEAD), jnp.float32))
        nv = jnp.sum(nv, axis=1, keepdims=True)
        wide = lax.broadcasted_iota(jnp.int32, (rows, slots * slot_len), 0) + j * tokens
        nv_send[...] += jnp.sum(jnp.where(tok_ref[...] == wide, nv, 0.0), axis=0, keepdims=True)
        return _

    lax.fori_loop(0, blocks, one_block, 0)

    own = pltpu.make_async_copy(
        send.at[blocks - 1, :, pl.ds((per_block - 1) * part, part)],
        recv_ref.at[blocks - 1, :, pl.ds((per_block - 1) * part, part)],
        self_sem,
    )
    own.start()
    trade = pltpu.make_async_remote_copy(
        src_ref=nv_send, dst_ref=nv_recv, send_sem=nv_send_sem, recv_sem=nv_recv_sem,
        device_id={"tensor": 1 - core}, device_id_type=MESH,
    )
    trade.start()
    trade.wait()
    wide = (slot_len, slots * slot_len)
    mine = lax.broadcasted_iota(jnp.int32, wide, 1) % slot_len == lax.broadcasted_iota(
        jnp.int32, wide, 0
    )
    tall = (slots * slot_len, slots)
    spread = jnp.where(
        lax.broadcasted_iota(jnp.int32, tall, 0) // slot_len
        == lax.broadcasted_iota(jnp.int32, tall, 1),
        1.0,
        0.0,
    )

    def fold(x):
        return jnp.dot(
            jnp.where(mine, x, 0.0), spread,
            precision=lax.Precision.HIGHEST, preferred_element_type=jnp.float32,
        )

    live = fold(jnp.where(tok_ref[...] >= 0, 1.0, 0.0))
    delta_ref[...] = jnp.where(
        live > 0.5, fold(nv_send[...] + nv_recv[...]) - old_ref[...], 0.0
    )
    own.wait()

    def finish(k, _):
        for g in range(pair_heads):
            outgoing(k, g).wait()
        return _

    lax.fori_loop(0, n - 1, finish, 0)


def place_kernel(rows, slot_len, order_ref, lo_ref, hi_ref, recv_ref, out_ref):
    tokens = BLOCK * slot_len
    blocks = out_ref.shape[0] // BLOCK

    def one_block(j, _):
        row = lax.broadcasted_iota(jnp.int32, (rows, tokens), 0)
        lo, hi = lo_ref[j], hi_ref[j]
        pick = jnp.where((lo == row) & (lo < hi), 1.0, 0.0).astype(jnp.bfloat16)
        half = recv_ref.shape[3]
        for g in range(recv_ref.shape[1]):
            full = lax.dot_general(
                pick, recv_ref[j, g], (((0,), (0,)), ((), ())), preferred_element_type=jnp.float32
            )
            for i in range(BLOCK):
                out_ref[order_ref[j * BLOCK + i], :, g * half : (g + 1) * half] = full[
                    i * slot_len : (i + 1) * slot_len
                ].astype(jnp.bfloat16)
        return _

    lax.fori_loop(0, blocks, one_block, 0)


def plan(partner, lens, me, n, rows, slot_len):
    slots = lens.shape[0]
    cap = slots // n
    per_block = BLOCK // cap
    slot = jnp.arange(slots, dtype=jnp.int32)
    earlier = (partner[:, None] == partner[None, :]) & (slot[None, :] < slot[:, None])
    rank = jnp.sum(earlier.astype(jnp.int32), axis=1)
    before = jnp.sum(jnp.where(earlier, lens[None, :], 0), axis=1)
    k = n - 1 - (partner ^ me)
    at = k * cap + rank
    first = (k % per_block) * (rows // per_block) + before
    match = at[None, :] == slot[:, None]

    def sort(x):
        return jnp.sum(jnp.where(match, x[None, :], 0), axis=1)

    position = jnp.arange(slot_len, dtype=jnp.int32)
    start = sort(first)
    lo = start[:, None] + position[None, :]
    hi = jnp.broadcast_to((start + sort(lens))[:, None], lo.shape)
    shape = (slots // BLOCK, 1, BLOCK * slot_len)
    token = jnp.where(
        position[None, :] < lens[:, None],
        ((k // per_block) * (BLOCK * slot_len) + first)[:, None] + position[None, :],
        -1,
    )
    return sort(slot), lo.reshape(shape), hi.reshape(shape), token.reshape(1, slots * slot_len)


def shards(queries, key_value_pairs, prompt_cache, score_weight, old_values, lengths, target_rank):
    me = lax.axis_index("dp").astype(jnp.int32)
    n = lax.axis_size("dp")
    slots, slot_len, width = queries.shape
    pair_heads = prompt_cache.shape[1] // (2 * HEAD)
    prompt_len = prompt_cache.shape[0]
    blocks = slots // BLOCK
    tokens = BLOCK * slot_len
    targets = target_rank.reshape(n, slots)
    lens = lengths.reshape(n, slots)
    my_targets = lax.dynamic_index_in_dim(targets, me, 0, keepdims=False)
    my_lens = lax.dynamic_index_in_dim(lens, me, 0, keepdims=False)
    arriving = targets == me
    ranks = jnp.arange(n, dtype=jnp.int32)
    source = jnp.sum(jnp.where(arriving, ranks[:, None], 0), axis=0)
    source_lens = jnp.sum(jnp.where(arriving, lens, 0), axis=0)
    order, lo, hi, token = plan(my_targets, my_lens, me, n, tokens, slot_len)
    in_order, in_lo, in_hi, _ = plan(source, source_lens, me, n, tokens, slot_len)

    smem = pl.BlockSpec(memory_space=pltpu.SMEM)
    vmem = pl.BlockSpec(memory_space=pltpu.VMEM)

    def attend(rows, call_id, operands, arrivals):
        half = width // pair_heads
        parcels = (blocks, pair_heads, rows, half)
        recv, delta = pl.pallas_call(
            functools.partial(score_kernel, n, rows, slot_len),
            out_shape=(
                jax.ShapeDtypeStruct(parcels, jnp.bfloat16),
                jax.ShapeDtypeStruct((slot_len, slots), jnp.float32),
            ),
            in_specs=[smem] + [vmem] * 8,
            out_specs=(pl.BlockSpec(memory_space=pl.ANY), vmem),
            scratch_shapes=[
                pltpu.VMEM((pair_heads, prompt_len + tokens, 2 * HEAD), jnp.bfloat16),
                pltpu.VMEM((pair_heads, prompt_len + tokens, 2 * HEAD), jnp.bfloat16),
                pltpu.VMEM((tokens, width), jnp.float32),
                pltpu.VMEM((tokens, prompt_cache.shape[1]), jnp.float32),
                pltpu.VMEM((rows, width), jnp.bfloat16),
                pltpu.VMEM(parcels, jnp.bfloat16),
                pltpu.VMEM((1, slots * slot_len), jnp.float32),
                pltpu.VMEM((1, slots * slot_len), jnp.float32),
                pltpu.SemaphoreType.DMA((n, pair_heads)),
                pltpu.SemaphoreType.DMA((n, pair_heads)),
                pltpu.SemaphoreType.DMA,
                pltpu.SemaphoreType.DMA,
                pltpu.SemaphoreType.DMA,
            ],
            compiler_params=pltpu.CompilerParams(
                collective_id=call_id, has_side_effects=True, vmem_limit_bytes=48 * 2**20
            ),
        )(*operands)
        attention = pl.pallas_call(
            functools.partial(place_kernel, rows, slot_len),
            out_shape=jax.ShapeDtypeStruct((slots, slot_len, width), jnp.bfloat16),
            in_specs=[smem, vmem, vmem, vmem],
            out_specs=vmem,
            compiler_params=pltpu.CompilerParams(vmem_limit_bytes=48 * 2**20),
        )(*arrivals, recv)
        return attention, delta

    operands = (order, lo, hi, token, queries, key_value_pairs, prompt_cache,
                score_weight.reshape(1, width), old_values.T)
    arrivals = (in_order, in_lo, in_hi)
    if n == blocks:
        pair = targets[:, None, :] == ranks[None, :, None]
        most = jnp.max(jnp.sum(jnp.where(pair, lens[:, None, :], 0), axis=2))
        mine, most = most.reshape(1), most.reshape(1)
        parts = lax.axis_size("group")
        for hop in range(1, parts):
            pairs = [(i, (i + hop) % parts) for i in range(parts)]
            most = jnp.maximum(most, lax.ppermute(mine, "group", pairs))
        most = most[0]
        sizes = [size for size in SIZES if size < tokens] + [tokens]
        choice = sum((most > size).astype(jnp.int32) for size in sizes[:-1])
        branches = [functools.partial(attend, size, i) for i, size in enumerate(sizes)]
        attention, delta = lax.switch(choice, branches, operands, arrivals)
    else:
        attention, delta = attend(tokens, 0, operands, arrivals)
    return attention, delta.T


def solution(mesh):
    placed = (
        P(("group", "dp"), None, "tensor"),
        P(("group", "dp"), None, "tensor"),
        P("group", "tensor"),
        P("tensor"),
        P(("group", "dp"), None),
        P("group"),
        P("group"),
    )
    return jax.shard_map(
        shards,
        mesh=mesh,
        in_specs=placed,
        out_specs=(P(("group", "dp"), None, "tensor"), P(("group", "dp"), None)),
        check_vma=False,
    )
```
